32 devices in a mesh: groups: 2 (over y), fsdp: 16 (over z, x, core).
Axes of the slice: x: 2, y: 2, z: 4, core: 2. Of those that a mesh axis runs over, the one named last changes fastest.
Arguments:
- grad_shards: bfloat16 [32, 512, 512], P('groups', 'fsdp'), parts along dimension 0, may hold values from -57 to 57
- offsets: int32 [32], P('groups'), parts along dimension 0, may hold values from 0 to 15, each once
- owners: int32 [32], P('groups'), parts along dimension 0, may hold values from 0 to 15, as said below
- left_stats: float32 [64, 512, 512], P(('groups', 'fsdp')), parts along dimension 0, may hold values from -0.4 to 8
- right_stats: float32 [64, 512, 512], P(('groups', 'fsdp')), parts along dimension 0, may hold values from -0.4 to 8
- left_root: bfloat16 [64, 512, 512], P(('groups', 'fsdp')), parts along dimension 0, may hold values from -0.11 to 1.21
- right_root: bfloat16 [64, 512, 512], P(('groups', 'fsdp')), parts along dimension 0, may hold values from -0.11 to 1.21
Outputs:
- update: bfloat16 [32, 512, 512], P('groups', 'fsdp'), parts along dimension 0
- new_left_stats: float32 [64, 512, 512], P(('groups', 'fsdp')), parts along dimension 0
- new_right_stats: float32 [64, 512, 512], P(('groups', 'fsdp')), parts along dimension 0
The draws below stay inside these ranges and needn't reach their ends.
There are 2 independent parts, one for each index of `groups`. The reference program is written for one: setup_inputs(seed, part) draws one part's arguments, and reference() takes and returns one part's arrays. A program takes and returns all parts, laid end to end along the dimension named above; each array names one. Nothing has to cross between parts.
Inputs may be any that keep to these rules, and one draw needn't show every extreme that they name: `owners`: every owner is named by at most 2 blocks, and some owner by exactly 2. Owners 2 k and 2 k + 1 are named by 2 blocks together, for every k.
All inputs are finite; a program needn't handle non-finite values.
Results may differ from the reference program's by a relative error of at most 0.0049.
Values may be sent and summed in bfloat16 or wider, within the bound.
A program may use at most 64 MiB of HBM per device.

```python
import jax
import jax.numpy as jnp
from jax import lax

BLOCK = 512
SLOTS = 2
BLOCKS = 16
N_FSDP = 16


def symmetric_draw(key, diag_lo, diag_hi, spread):
    first, second = jax.random.split(key)
    full_shape = (N_FSDP * SLOTS, BLOCK, BLOCK)
    noise = jax.random.truncated_normal(first, -4.0, 4.0, full_shape, jnp.float32)
    mirrored = (noise + jnp.swapaxes(noise, 1, 2)) * (spread * 0.7071)
    diagonal = jnp.exp(jax.random.uniform(second, (N_FSDP * SLOTS, BLOCK), jnp.float32, jnp.log(diag_lo), jnp.log(diag_hi)))
    identity = jnp.eye(BLOCK, dtype=jnp.float32)
    return mirrored * (1.0 - identity) + diagonal[:, :, None] * identity


def draw_grad_shards(key, part):
    key = jax.random.fold_in(key, 5)
    subkeys = jax.random.split(key, 3)
    full_shape = (BLOCKS, BLOCK, BLOCK)
    position = jnp.arange(BLOCK, dtype=jnp.float32) / BLOCK - 0.5
    row_scale = 10.0 ** position[None, :, None] * 2.0 ** (jax.random.uniform(subkeys[1], (BLOCKS, BLOCK, 1), jnp.float32) - 0.5)
    col_scale = 10.0 ** (jax.random.uniform(subkeys[2], (BLOCKS, 1, BLOCK), jnp.float32) - 0.5)
    values = jax.random.truncated_normal(subkeys[0], -4.0, 4.0, full_shape, jnp.float32)
    return (values * row_scale * col_scale).astype(jnp.bfloat16)


def draw_owners(key, part):
    key = jax.random.fold_in(key, 7)
    subkeys = jax.random.split(key, 4)
    pair_count = N_FSDP // 2
    split_pair = jax.random.randint(subkeys[0], (pair_count,), 0, 2).astype(jnp.int32)
    heavy_side = jax.random.randint(subkeys[1], (pair_count,), 0, 2).astype(jnp.int32)
    split_pair = split_pair.at[0].set(1)
    first_load = jnp.where(split_pair == 1, 2 * heavy_side, 1).astype(jnp.int32)
    owner_loads = jnp.stack([first_load, 2 - first_load], axis=1).reshape(-1)
    pair_order = jax.random.permutation(subkeys[2], pair_count).astype(jnp.int32)
    relabel = (2 * pair_order[:, None] + jnp.arange(2, dtype=jnp.int32)[None, :]).reshape(-1).astype(jnp.int32)
    load_ends = jnp.cumsum(owner_loads)
    positions = jnp.arange(BLOCKS, dtype=jnp.int32)
    holder = jnp.sum((load_ends[None, :] <= positions[:, None]).astype(jnp.int32), axis=1)
    shuffle = jax.random.permutation(subkeys[3], BLOCKS)
    return jnp.zeros((BLOCKS,), jnp.int32).at[shuffle].set(relabel[holder]).astype(jnp.int32)


def draw_left_stats(key, part):
    key = jax.random.fold_in(key, 11)
    return symmetric_draw(key, 0.5, 8.0, 0.05)


def draw_right_stats(key, part):
    key = jax.random.fold_in(key, 13)
    return symmetric_draw(key, 0.5, 8.0, 0.05)


def draw_left_root(key, part):
    key = jax.random.fold_in(key, 17)
    return symmetric_draw(key, 0.5, 1.2, 0.2 / BLOCK ** 0.5).astype(jnp.bfloat16)


def draw_right_root(key, part):
    key = jax.random.fold_in(key, 19)
    return symmetric_draw(key, 0.5, 1.2, 0.2 / BLOCK ** 0.5).astype(jnp.bfloat16)


def setup_inputs(seed: int = 0, part: int = 0) -> dict:
    arg_keys = jax.random.split(jax.random.key(seed), 8)
    part_keys = jax.random.split(jax.random.fold_in(arg_keys[7], part), 8)
    return {
        "grad_shards": draw_grad_shards(jax.random.fold_in(jax.random.fold_in(arg_keys[7], part), 71), part),
        "offsets": jax.random.permutation(part_keys[1], BLOCKS).astype(jnp.int32),
        "owners": draw_owners(jax.random.fold_in(jax.random.fold_in(arg_keys[7], part), 71), part),
        "left_stats": draw_left_stats(jax.random.fold_in(jax.random.fold_in(arg_keys[7], part), 71), part),
        "right_stats": draw_right_stats(jax.random.fold_in(jax.random.fold_in(arg_keys[7], part), 71), part),
        "left_root": draw_left_root(jax.random.fold_in(jax.random.fold_in(arg_keys[7], part), 71), part),
        "right_root": draw_right_root(jax.random.fold_in(jax.random.fold_in(arg_keys[7], part), 71), part),
    }


DECAY = 0.999
CLIP_RMS = 1.0
EPSILON = 1e-06

def slot_tables(owners, peer_count, capacity):
    block_count = owners.shape[0]
    block_ids = jnp.arange(block_count, dtype=jnp.int32)
    same_owner = owners[None, :] == owners[:, None]
    earlier = block_ids[None, :] < block_ids[:, None]
    slot_rank = lax.optimization_barrier(jnp.sum((same_owner & earlier).astype(jnp.int32), axis=1)).astype(jnp.int32)
    slot_ids = jnp.arange(capacity, dtype=jnp.int32)
    holder_ids = jnp.arange(peer_count, dtype=jnp.int32)
    slot_match = (owners[None, None, :] == holder_ids[None, :, None]) & (slot_rank[None, None, :] == slot_ids[:, None, None])
    return (slot_rank, slot_match)

def precondition(gradient, grad_mean, left_old, right_old, left_inv, right_inv, clip_factor):
    left_new = DECAY * left_old + (1.0 - DECAY) * jnp.dot(gradient, gradient.T, preferred_element_type=jnp.float32)
    right_new = DECAY * right_old + (1.0 - DECAY) * jnp.dot(gradient.T, gradient, preferred_element_type=jnp.float32)
    left_half = jnp.dot(left_inv, gradient, preferred_element_type=jnp.float32).astype(jnp.bfloat16)
    direction = jnp.dot(left_half, right_inv, preferred_element_type=jnp.float32)
    graft_scale = jnp.sqrt(grad_mean / (jnp.mean(direction * direction) + EPSILON))
    return (left_new, right_new, (clip_factor * (graft_scale * direction)).astype(jnp.bfloat16))

def reference(grad_shards, offsets, owners, left_stats, right_stats, left_root, right_root):
    block_count = grad_shards.shape[0]
    block_size = grad_shards.shape[2]
    slot_rank, slot_match = slot_tables(owners, N_FSDP, SLOTS)
    by_owner = jnp.swapaxes(slot_match.astype(jnp.int32), 0, 1).reshape(N_FSDP * SLOTS, block_count)
    block_ids = jnp.arange(block_count, dtype=jnp.int32)
    holder = lax.optimization_barrier(jnp.sum(by_owner * block_ids[None, :], axis=1)).astype(jnp.int32)
    filled = lax.optimization_barrier(jnp.sum(by_owner, axis=1)).astype(jnp.int32)
    block_grad = grad_shards[offsets]
    widened = grad_shards.astype(jnp.float32)
    square_mean = jnp.sum(widened * widened) / (block_count * block_size * block_size)
    clip_factor = jnp.minimum(1.0, CLIP_RMS * lax.rsqrt(square_mean))

    def one_slot(slot_inputs):
        holder_index, occupied, left_old, right_old, left_inv, right_inv = slot_inputs
        gradient = jnp.where(occupied > 0, block_grad[holder_index], jnp.zeros((block_size, block_size), block_grad.dtype))
        wide_grad = gradient.astype(jnp.float32)
        return precondition(gradient, jnp.mean(wide_grad * wide_grad), left_old, right_old, left_inv, right_inv, clip_factor)
    left_new, right_new, slot_update = lax.map(one_slot, (holder, filled, left_stats, right_stats, left_root, right_root))
    slot_of_block = (owners * SLOTS + slot_rank).astype(jnp.int32)
    update = jnp.zeros_like(grad_shards).at[offsets].set(slot_update[slot_of_block])
    return (update, left_new, right_new)
```

```python
import functools

import jax
import jax.numpy as jnp
from jax import lax
from jax.experimental import pallas as pl
from jax.experimental.pallas import tpu as pltpu
from jax.sharding import PartitionSpec as P

DECAY = 0.999
CLIP_RMS = 1.0
EPSILON = 1e-06


def slot_tables(owners, peer_count, capacity):
    block_count = owners.shape[0]
    block_ids = jnp.arange(block_count, dtype=jnp.int32)
    same_owner = owners[None, :] == owners[:, None]
    earlier = block_ids[None, :] < block_ids[:, None]
    slot_rank = jnp.sum((same_owner & earlier).astype(jnp.int32), axis=1)
    slot_ids = jnp.arange(capacity, dtype=jnp.int32)
    holder_ids = jnp.arange(peer_count, dtype=jnp.int32)
    slot_match = (owners[None, None, :] == holder_ids[None, :, None]) & (
        slot_rank[None, None, :] == slot_ids[:, None, None]
    )
    return (slot_rank, slot_match)


def precondition(gradient, grad_mean, left_old, right_old, left_inv, right_inv, clip_factor):
    left_new = DECAY * left_old + (1.0 - DECAY) * jnp.dot(
        gradient, gradient.T, preferred_element_type=jnp.float32
    )
    right_new = DECAY * right_old + (1.0 - DECAY) * jnp.dot(
        gradient.T, gradient, preferred_element_type=jnp.float32
    )
    left_half = jnp.dot(left_inv, gradient, preferred_element_type=jnp.float32).astype(jnp.bfloat16)
    direction = jnp.dot(left_half, right_inv, preferred_element_type=jnp.float32)
    graft_scale = jnp.sqrt(grad_mean / (jnp.mean(direction * direction) + EPSILON))
    return (left_new, right_new, (clip_factor * (graft_scale * direction)).astype(jnp.bfloat16))


def padded_body(grad_shards, offsets, owners, left_stats, right_stats, left_root, right_root):
    peer_count = lax.axis_size("fsdp")
    capacity = left_stats.shape[0]
    block_count, strip_rows, block_size = grad_shards.shape
    slot_rank, slot_match = slot_tables(owners, peer_count, capacity)
    positions = jnp.arange(block_count, dtype=jnp.int32)
    at_position = (offsets[None, :] == positions[:, None]).astype(jnp.int32)
    matched = slot_match.astype(jnp.int32)
    source_rows = jnp.sum(matched * offsets[None, None, :], axis=2).reshape(-1)
    occupied = jnp.sum(matched, axis=2).reshape(-1)
    picked = jnp.take(grad_shards, source_rows, axis=0)
    picked = jnp.where(occupied[:, None, None] > 0, picked, jnp.zeros_like(picked))
    outgoing = picked.reshape(capacity, peer_count * strip_rows, block_size)
    arrived = lax.all_to_all(outgoing, "fsdp", split_axis=1, concat_axis=1, tiled=True)
    widened = arrived.astype(jnp.float32)
    slot_squares = jnp.sum(widened * widened, axis=(1, 2))
    entries = block_count * block_size * block_size
    local_grad = grad_shards.astype(jnp.float32)
    square_sum = lax.psum(jnp.sum(local_grad * local_grad), "fsdp")
    clip_factor = jnp.minimum(1.0, CLIP_RMS * lax.rsqrt(square_sum / entries))
    left_list = []
    right_list = []
    update_list = []
    for slot_index in range(capacity):
        grad_mean = slot_squares[slot_index] / (block_size * block_size)
        left_new, right_new, slot_update = precondition(
            arrived[slot_index],
            grad_mean,
            left_stats[slot_index],
            right_stats[slot_index],
            left_root[slot_index],
            right_root[slot_index],
            clip_factor,
        )
        left_list.append(left_new)
        right_list.append(right_new)
        update_list.append(slot_update)
    slot_updates = jnp.stack(update_list)
    returned = lax.all_to_all(slot_updates, "fsdp", split_axis=1, concat_axis=1, tiled=True)
    anchor = slot_rank * peer_count + owners
    where_from = jnp.sum(at_position * anchor[None, :], axis=1)
    update = jnp.take(
        returned.reshape(capacity * peer_count, strip_rows, block_size), where_from, axis=0
    )
    return (update, jnp.stack(left_list), jnp.stack(right_list))


AXIS = "fsdp"
MESH = pl.DeviceIdType.MESH


def exchange_kernel(
    n,
    offsets_ref,
    owners_ref,
    grad_hbm,
    left_hbm,
    right_hbm,
    returned_ref,
    slot_grad_ref,
    table_ref,
    grad_ref,
    outgoing_ref,
    blocks_ref,
    left_ref,
    right_ref,
    update_ref,
    sums_ref,
    local_sem,
    strip_send,
    strip_recv,
    sum_send,
    sum_recv,
    back_send,
    back_recv,
    pair_send,
    pair_recv,
):
    strip = grad_ref.shape[1]
    block_size = grad_ref.shape[2]
    capacity = left_hbm.shape[0]
    me = lax.axis_index(AXIS)
    side = lax.rem(me, 2)
    pair = me // 2
    sibling = me + 1 - 2 * side

    def peer(step):
        return lax.rem(me + lax.rem(step * 7, n), n)

    def rows_of(device):
        return pl.ds(pl.multiple_of(device * strip, strip), strip)

    def strip_copy(source, target):
        return pltpu.make_async_remote_copy(
            src_ref=outgoing_ref.at[target],
            dst_ref=blocks_ref.at[lax.rem(target, 2), rows_of(source)],
            send_sem=strip_send.at[target],
            recv_sem=strip_recv.at[source],
            device_id={AXIS: target},
            device_id_type=MESH,
        )

    def sum_copy(source, target):
        return pltpu.make_async_remote_copy(
            src_ref=sums_ref.at[source],
            dst_ref=sums_ref.at[source],
            send_sem=sum_send.at[target],
            recv_sem=sum_recv.at[source],
            device_id={AXIS: target},
            device_id_type=MESH,
        )

    def back_copy(source, target):
        return pltpu.make_async_remote_copy(
            src_ref=update_ref.at[rows_of(target)],
            dst_ref=returned_ref.at[source],
            send_sem=back_send.at[target],
            recv_sem=back_recv.at[source],
            device_id={AXIS: target},
            device_id_type=MESH,
        )

    def pair_copy(index, source, target):
        return pltpu.make_async_remote_copy(
            src_ref=source,
            dst_ref=target,
            send_sem=pair_send.at[index],
            recv_sem=pair_recv.at[index],
            device_id={AXIS: sibling},
            device_id_type=MESH,
        )

    def each_peer(action):
        def step(index, carry):
            action(peer(index))
            return carry

        lax.fori_loop(1, n, step, 0)

    barrier = pltpu.get_barrier_semaphore()
    each_peer(
        lambda other: pl.semaphore_signal(
            barrier, inc=1, device_id={AXIS: other}, device_id_type=MESH
        )
    )
    own_slots = pl.ds(side * capacity, capacity)
    other_slots = pl.ds((1 - side) * capacity, capacity)
    grad_load = pltpu.make_async_copy(grad_hbm, grad_ref, local_sem.at[0])
    left_load = pltpu.make_async_copy(left_hbm, left_ref.at[own_slots], local_sem.at[1])
    right_load = pltpu.make_async_copy(right_hbm, right_ref.at[own_slots], local_sem.at[2])
    grad_load.start()
    left_load.start()
    right_load.start()

    owners = [owners_ref[b] for b in range(n)]
    offsets = [offsets_ref[b] for b in range(n)]
    pairs = [owner // 2 for owner in owners]
    for k in range(n // 2):
        first = offsets[0]
        last = offsets[0]
        for b in range(1, n):
            last = jnp.where(pairs[b] == k, offsets[b], last)
        for b in range(n - 1, -1, -1):
            first = jnp.where(pairs[b] == k, offsets[b], first)
        table_ref[2 * k] = first
        table_ref[2 * k + 1] = last
    first_owner = owners[0]
    last_owner = owners[0]
    for b in range(1, n):
        last_owner = jnp.where(pairs[b] == pair, owners[b], last_owner)
    for b in range(n - 1, -1, -1):
        first_owner = jnp.where(pairs[b] == pair, owners[b], first_owner)
    same = first_owner == last_owner
    first_side = lax.rem(first_owner, 2)
    last_side = lax.rem(last_owner, 2)
    last_rank = jnp.where(same, 1, 0)
    chosen = jnp.where(side == 0, first_side * capacity, last_side * capacity + last_rank)

    grad_load.wait()
    pl.semaphore_wait(barrier, n - 1)

    def send_strip(other):
        outgoing_ref[other] = grad_ref[table_ref[other]]
        strip_copy(me, other).start()

    each_peer(send_strip)

    squares = jnp.zeros((strip, block_size), jnp.float32)
    for b in range(n):
        wide = grad_ref[b].astype(jnp.float32)
        squares += wide * wide
    partial = squares[0:8]
    for r in range(8, strip, 8):
        partial += squares[r : r + 8]
    lanes = partial[:, 0:128]
    for c in range(128, block_size, 128):
        lanes += partial[:, c : c + 128]
    sums_ref[me] = lanes
    each_peer(lambda other: sum_copy(me, other).start())

    left_swap = pair_copy(0, left_hbm, left_ref.at[own_slots])
    right_swap = pair_copy(1, right_hbm, right_ref.at[own_slots])
    left_swap.start()
    right_swap.start()
    blocks_ref[side, rows_of(me)] = grad_ref[table_ref[me]]

    each_peer(lambda other: sum_copy(other, me).wait_recv())
    total = jnp.sum(jnp.sum(sums_ref[...], axis=0), axis=(0, 1), keepdims=True)
    entries = n * block_size * block_size
    clip_factor = jnp.minimum(1.0, CLIP_RMS * lax.rsqrt(total / entries))
    left_load.wait()
    right_load.wait()
    pair_copy(0, left_hbm, left_ref.at[other_slots]).wait_recv()
    pair_copy(1, right_hbm, right_ref.at[other_slots]).wait_recv()

    each_peer(lambda other: strip_copy(other, me).wait_recv())
    block_swap = pair_copy(2, blocks_ref.at[side], blocks_ref.at[side])
    block_swap.start()

    block = blocks_ref[side]
    wide = block.astype(jnp.float32)
    grad_mean = jnp.sum(wide * wide, axis=(0, 1), keepdims=True) / (block_size * block_size)
    left_half = jnp.dot(left_ref[chosen], block, preferred_element_type=jnp.float32)
    direction = jnp.dot(
        left_half.astype(jnp.bfloat16), right_ref[chosen], preferred_element_type=jnp.float32
    )
    direction_mean = jnp.sum(direction * direction, axis=(0, 1), keepdims=True) / (
        block_size * block_size
    )
    graft_scale = jnp.sqrt(grad_mean / (direction_mean + EPSILON))
    update_ref[...] = (clip_factor * (graft_scale * direction)).astype(jnp.bfloat16)
    each_peer(lambda other: back_copy(me, other).start())
    returned_ref[me] = update_ref[rows_of(me)]

    pair_copy(2, blocks_ref.at[1 - side], blocks_ref.at[1 - side]).wait_recv()
    for s in range(capacity):
        from_first = (first_side == side) & (s == 0)
        from_last = (last_side == side) & (last_rank == s)
        index = jnp.where(from_last, 1, 0)
        filled = jnp.where(from_first | from_last, 1.0, 0.0).astype(jnp.bfloat16)
        slot_grad_ref[s] = blocks_ref[index] * filled

    left_swap.wait_send()
    right_swap.wait_send()
    block_swap.wait_send()
    each_peer(lambda other: strip_copy(me, other).wait_send())
    each_peer(lambda other: sum_copy(me, other).wait_send())
    each_peer(lambda other: back_copy(other, me).wait_recv())
    each_peer(lambda other: back_copy(me, other).wait_send())


def exchange(n, grad_shards, offsets, owners, left_root, right_root):
    blocks, strip, size = grad_shards.shape
    capacity = left_root.shape[0]
    half = jnp.bfloat16
    vmem = pl.BlockSpec(memory_space=pltpu.VMEM)
    smem = pl.BlockSpec(memory_space=pltpu.SMEM)
    anywhere = pl.BlockSpec(memory_space=pl.ANY)
    many = pltpu.SemaphoreType.DMA((n,))
    few = pltpu.SemaphoreType.DMA((3,))
    return pl.pallas_call(
        functools.partial(exchange_kernel, n),
        out_shape=(
            jax.ShapeDtypeStruct((n, strip, size), half),
            jax.ShapeDtypeStruct((capacity, size, size), half),
            jax.ShapeDtypeStruct((n,), jnp.int32),
        ),
        in_specs=[smem, smem, anywhere, anywhere, anywhere],
        out_specs=(vmem, vmem, smem),
        scratch_shapes=[
            pltpu.VMEM((blocks, strip, size), half),
            pltpu.VMEM((n, strip, size), half),
            pltpu.VMEM((2, size, size), half),
            pltpu.VMEM((2 * capacity, size, size), half),
            pltpu.VMEM((2 * capacity, size, size), half),
            pltpu.VMEM((size, size), half),
            pltpu.VMEM((n, 8, 128), jnp.float32),
            few,
            many,
            many,
            many,
            many,
            many,
            many,
            few,
            few,
        ],
        compiler_params=pltpu.CompilerParams(
            collective_id=0, has_side_effects=True, vmem_limit_bytes=24 * 1024 * 1024
        ),
        cost_estimate=pl.CostEstimate(
            flops=4 * size**3, bytes_accessed=100 * 1024 * 1024, transcendentals=0
        ),
        name="exchange",
    )(offsets, owners, grad_shards, left_root, right_root)


def statistics_kernel(
    table_ref, returned_ref, slot_ref, left_ref, right_ref, update_ref, left_out, right_out
):
    tile = left_ref.shape[1]
    part = pl.program_id(1)

    @pl.when((pl.program_id(0) == 0) & (part == 0))
    def _():
        for d in range(returned_ref.shape[0]):
            update_ref[table_ref[d]] = returned_ref[d]

    span = pl.ds(pl.multiple_of(part * tile, tile), tile)
    gradient = slot_ref[0]
    rows = slot_ref[0, span, :]
    columns = slot_ref[0, :, span]
    left_out[0] = DECAY * left_ref[0] + (1.0 - DECAY) * lax.dot_general(
        rows, gradient, (((1,), (1,)), ((), ())), preferred_element_type=jnp.float32
    )
    right_out[0] = DECAY * right_ref[0] + (1.0 - DECAY) * lax.dot_general(
        columns, gradient, (((0,), (0,)), ((), ())), preferred_element_type=jnp.float32
    )


def statistics(table, returned, slot_grad, left_stats, right_stats):
    capacity, size, _ = left_stats.shape
    tile = size // 2
    whole = pl.BlockSpec(returned.shape, lambda s, p, t: (0, 0, 0))
    tiled = pl.BlockSpec((1, tile, size), lambda s, p, t: (s, p, 0))
    return pl.pallas_call(
        statistics_kernel,
        grid_spec=pltpu.PrefetchScalarGridSpec(
            num_scalar_prefetch=1,
            grid=(capacity, size // tile),
            in_specs=[
                whole,
                pl.BlockSpec((1, size, size), lambda s, p, t: (s, 0, 0)),
                tiled,
                tiled,
            ],
            out_specs=[whole, tiled, tiled],
        ),
        out_shape=(
            jax.ShapeDtypeStruct(returned.shape, returned.dtype),
            jax.ShapeDtypeStruct(left_stats.shape, jnp.float32),
            jax.ShapeDtypeStruct(right_stats.shape, jnp.float32),
        ),
        compiler_params=pltpu.CompilerParams(vmem_limit_bytes=24 * 1024 * 1024),
        cost_estimate=pl.CostEstimate(
            flops=4 * capacity * size**3,
            bytes_accessed=16 * capacity * size * size,
            transcendentals=0,
        ),
        name="statistics",
    )(table, returned, slot_grad, left_stats, right_stats)


def body(grad_shards, offsets, owners, left_stats, right_stats, left_root, right_root):
    n = lax.axis_size(AXIS)
    blocks, strip, _ = grad_shards.shape
    if blocks != n or strip % 16 or left_stats.shape[0] != 2:
        return padded_body(
            grad_shards, offsets, owners, left_stats, right_stats, left_root, right_root
        )
    returned, slot_grad, table = exchange(
        n, grad_shards, offsets, owners, left_root, right_root
    )
    return statistics(table, returned, slot_grad, left_stats, right_stats)


def solution(mesh):
    placed = (
        P("groups", "fsdp", None),
        P("groups"),
        P("groups"),
        P(("groups", "fsdp"), None, None),
        P(("groups", "fsdp"), None, None),
        P(("groups", "fsdp"), None, None),
        P(("groups", "fsdp"), None, None),
    )
    return jax.shard_map(
        body,
        mesh=mesh,
        in_specs=placed,
        out_specs=(
            P("groups", "fsdp", None),
            P(("groups", "fsdp"), None, None),
            P(("groups", "fsdp"), None, None),
        ),
        check_vma=False,
    )
```

```python
import functools

import jax
import jax.numpy as jnp
from jax import lax
from jax.experimental import pallas as pl
from jax.experimental.pallas import tpu as pltpu
from jax.sharding import PartitionSpec as P

DECAY = 0.999
CLIP_RMS = 1.0
EPSILON = 1e-06


def slot_tables(owners, peer_count, capacity):
    block_count = owners.shape[0]
    block_ids = jnp.arange(block_count, dtype=jnp.int32)
    same_owner = owners[None, :] == owners[:, None]
    earlier = block_ids[None, :] < block_ids[:, None]
    slot_rank = jnp.sum((same_owner & earlier).astype(jnp.int32), axis=1)
    slot_ids = jnp.arange(capacity, dtype=jnp.int32)
    holder_ids = jnp.arange(peer_count, dtype=jnp.int32)
    slot_match = (owners[None, None, :] == holder_ids[None, :, None]) & (
        slot_rank[None, None, :] == slot_ids[:, None, None]
    )
    return (slot_rank, slot_match)


def precondition(gradient, grad_mean, left_old, right_old, left_inv, right_inv, clip_factor):
    left_new = DECAY * left_old + (1.0 - DECAY) * jnp.dot(
        gradient, gradient.T, preferred_element_type=jnp.float32
    )
    right_new = DECAY * right_old + (1.0 - DECAY) * jnp.dot(
        gradient.T, gradient, preferred_element_type=jnp.float32
    )
    left_half = jnp.dot(left_inv, gradient, preferred_element_type=jnp.float32).astype(jnp.bfloat16)
    direction = jnp.dot(left_half, right_inv, preferred_element_type=jnp.float32)
    graft_scale = jnp.sqrt(grad_mean / (jnp.mean(direction * direction) + EPSILON))
    return (left_new, right_new, (clip_factor * (graft_scale * direction)).astype(jnp.bfloat16))


def padded_body(grad_shards, offsets, owners, left_stats, right_stats, left_root, right_root):
    peer_count = lax.axis_size("fsdp")
    capacity = left_stats.shape[0]
    block_count, strip_rows, block_size = grad_shards.shape
    slot_rank, slot_match = slot_tables(owners, peer_count, capacity)
    positions = jnp.arange(block_count, dtype=jnp.int32)
    at_position = (offsets[None, :] == positions[:, None]).astype(jnp.int32)
    matched = slot_match.astype(jnp.int32)
    source_rows = jnp.sum(matched * offsets[None, None, :], axis=2).reshape(-1)
    occupied = jnp.sum(matched, axis=2).reshape(-1)
    picked = jnp.take(grad_shards, source_rows, axis=0)
    picked = jnp.where(occupied[:, None, None] > 0, picked, jnp.zeros_like(picked))
    outgoing = picked.reshape(capacity, peer_count * strip_rows, block_size)
    arrived = lax.all_to_all(outgoing, "fsdp", split_axis=1, concat_axis=1, tiled=True)
    widened = arrived.astype(jnp.float32)
    slot_squares = jnp.sum(widened * widened, axis=(1, 2))
    entries = block_count * block_size * block_size
    local_grad = grad_shards.astype(jnp.float32)
    square_sum = lax.psum(jnp.sum(local_grad * local_grad), "fsdp")
    clip_factor = jnp.minimum(1.0, CLIP_RMS * lax.rsqrt(square_sum / entries))
    left_list = []
    right_list = []
    update_list = []
    for slot_index in range(capacity):
        grad_mean = slot_squares[slot_index] / (block_size * block_size)
        left_new, right_new, slot_update = precondition(
            arrived[slot_index],
            grad_mean,
            left_stats[slot_index],
            right_stats[slot_index],
            left_root[slot_index],
            right_root[slot_index],
            clip_factor,
        )
        left_list.append(left_new)
        right_list.append(right_new)
        update_list.append(slot_update)
    slot_updates = jnp.stack(update_list)
    returned = lax.all_to_all(slot_updates, "fsdp", split_axis=1, concat_axis=1, tiled=True)
    anchor = slot_rank * peer_count + owners
    where_from = jnp.sum(at_position * anchor[None, :], axis=1)
    update = jnp.take(
        returned.reshape(capacity * peer_count, strip_rows, block_size), where_from, axis=0
    )
    return (update, jnp.stack(left_list), jnp.stack(right_list))


AXIS = "fsdp"
MESH = pl.DeviceIdType.MESH


def mean_square(values):
    return jnp.sum(values * values, axis=(0, 1), keepdims=True) / values.size


def exchange_kernel(
    n,
    offsets_hbm,
    owners_hbm,
    grad_hbm,
    left_hbm,
    right_hbm,
    left_root_hbm,
    right_root_hbm,
    update_ref,
    left_out,
    right_out,
    offsets_ref,
    owners_ref,
    table_ref,
    place_ref,
    grad_ref,
    outgoing_ref,
    blocks_ref,
    left_root_ref,
    right_root_ref,
    root_out_ref,
    root_in_ref,
    root_ref,
    slot_update_ref,
    returned_ref,
    slot_grad_ref,
    left_ref,
    right_ref,
    sums_ref,
    local_sem,
    stat_sem,
    strip_send,
    strip_recv,
    sum_send,
    sum_recv,
    back_send,
    back_recv,
    pair_send,
    pair_recv,
):
    strip, block_size = grad_ref.shape[1:]
    capacity = left_root_hbm.shape[0]
    pair_count = n // 2
    me = lax.axis_index(AXIS)
    pair = me // 2
    side = me - 2 * pair
    sibling = me + 1 - 2 * side

    def wrapped(k):
        ahead = pair + k
        return jnp.where(ahead >= pair_count, ahead - pair_count, ahead)

    middle = pair_count // 2
    steps = sorted(range(1, pair_count), key=lambda k: (abs(k - middle), k))
    to_first = [2 * wrapped(k) for k in steps]
    to_last = [2 * wrapped(k) + 1 for k in steps]
    others = to_first + to_last + [sibling]

    def rows_of(device):
        return pl.ds(pl.multiple_of(device * strip, strip), strip)

    def remote(source, target, send_sem, recv_sem, device):
        return pltpu.make_async_remote_copy(
            src_ref=source,
            dst_ref=target,
            send_sem=send_sem,
            recv_sem=recv_sem,
            device_id={AXIS: device},
            device_id_type=MESH,
        )

    def strip_copy(source, target):
        return remote(
            outgoing_ref.at[target],
            blocks_ref.at[target - 2 * (target // 2), rows_of(source)],
            strip_send.at[target],
            strip_recv.at[source],
            target,
        )

    def sum_copy(source, target):
        row = sums_ref.at[source]
        return remote(row, row, sum_send.at[target], sum_recv.at[source], target)

    def back_copy(source, target):
        return remote(
            slot_update_ref.at[rows_of(target)],
            returned_ref.at[source],
            back_send.at[target],
            back_recv.at[source],
            target,
        )

    def pair_copy(index, source, target):
        return remote(source, target, pair_send.at[index], pair_recv.at[index], sibling)

    barrier = pltpu.get_barrier_semaphore()
    for other in others:
        pl.semaphore_signal(barrier, inc=1, device_id={AXIS: other}, device_id_type=MESH)
    loads = [
        pltpu.make_async_copy(source, target, local_sem.at[i])
        for i, (source, target) in enumerate(
            [
                (offsets_hbm, offsets_ref),
                (owners_hbm, owners_ref),
                (grad_hbm, grad_ref),
                (left_root_hbm, left_root_ref),
                (right_root_hbm, right_root_ref),
                (left_hbm, left_ref),
                (right_hbm, right_ref),
            ]
        )
    ]
    for load in loads[:5]:
        load.start()

    loads[0].wait()
    loads[1].wait()
    owners = [owners_ref[b] for b in range(n)]
    offsets = [offsets_ref[b] for b in range(n)]
    pairs = [owner >> 1 for owner in owners]
    for k in range(pair_count):
        first = offsets[0]
        last = offsets[0]
        for b in range(1, n):
            last = jnp.where(pairs[b] == k, offsets[b], last)
        for b in range(n - 1, -1, -1):
            first = jnp.where(pairs[b] == k, offsets[b], first)
        table_ref[2 * k] = first
        table_ref[2 * k + 1] = last
    first_owner = owners[0]
    last_owner = owners[0]
    for b in range(1, n):
        last_owner = jnp.where(pairs[b] == pair, owners[b], last_owner)
    for b in range(n - 1, -1, -1):
        first_owner = jnp.where(pairs[b] == pair, owners[b], first_owner)
    first_side = first_owner & 1
    last_side = last_owner & 1
    last_rank = jnp.where(first_owner == last_owner, 1, 0)
    my_side = jnp.where(side == 0, first_side, last_side)
    my_rank = jnp.where(side == 0, 0, last_rank)
    sibling_rank = jnp.where(side == 0, last_rank, 0)
    own_root = my_side == side

    loads[2].wait()
    squares = jnp.zeros((strip, block_size), jnp.float32)
    for b in range(n):
        wide = grad_ref[b].astype(jnp.float32)
        squares += wide * wide
    partial = squares[0:8]
    for r in range(8, strip, 8):
        partial += squares[r : r + 8]
    lanes = partial[:, 0:128]
    for c in range(128, block_size, 128):
        lanes += partial[:, c : c + 128]
    sums_ref[me] = lanes
    pl.semaphore_wait(barrier, n - 1)

    def send_strip(other):
        outgoing_ref[other] = grad_ref[table_ref[other]]
        strip_copy(me, other).start()

    for other in to_first:
        send_strip(other)
    for other in others:
        sum_copy(me, other).start()
    send_strip(sibling)
    for other in to_last:
        send_strip(other)
    blocks_ref[side, rows_of(me)] = grad_ref[table_ref[me]]

    loads[3].wait()
    root_out_ref[0] = left_root_ref[sibling_rank]
    left_swap = pair_copy(0, root_out_ref.at[0], root_in_ref.at[0])
    left_swap.start()
    loads[4].wait()
    root_out_ref[1] = right_root_ref[sibling_rank]
    right_swap = pair_copy(1, root_out_ref.at[1], root_in_ref.at[1])
    right_swap.start()
    loads[5].start()
    loads[6].start()

    for other in others:
        sum_copy(other, me).wait_recv()
    total = jnp.sum(jnp.sum(sums_ref[...], axis=0), axis=(0, 1), keepdims=True)
    clip_factor = jnp.minimum(1.0, CLIP_RMS * lax.rsqrt(total / (n * block_size * block_size)))
    left_swap.wait_recv()
    right_swap.wait_recv()
    root_ref[0] = jnp.where(own_root, left_root_ref[my_rank], root_in_ref[0])
    root_ref[1] = jnp.where(own_root, right_root_ref[my_rank], root_in_ref[1])

    for other in others:
        strip_copy(other, me).wait_recv()
    block_swap = pair_copy(2, blocks_ref.at[side], blocks_ref.at[side])
    block_swap.start()

    block = blocks_ref[side]
    grad_mean = mean_square(block.astype(jnp.float32))
    left_half = jnp.dot(root_ref[0], block, preferred_element_type=jnp.float32)
    direction = jnp.dot(
        left_half.astype(jnp.bfloat16),
        root_ref[1],
        preferred_element_type=jnp.float32,
    )
    graft_scale = jnp.sqrt(grad_mean / (mean_square(direction) + EPSILON))
    slot_update_ref[...] = (clip_factor * (graft_scale * direction)).astype(jnp.bfloat16)
    for other in others:
        back_copy(me, other).start()
    returned_ref[me] = slot_update_ref[rows_of(me)]

    for p in range(n):
        holder = 0
        for d in range(n):
            holder = jnp.where(table_ref[d] == p, d, holder)
        place_ref[p] = holder

    loads[5].wait()
    loads[6].wait()
    pair_copy(2, blocks_ref.at[1 - side], blocks_ref.at[1 - side]).wait_recv()
    stores = []
    for s in range(capacity):
        from_first = (first_side == side) & (s == 0)
        from_last = (last_side == side) & (last_rank == s)
        index = jnp.where(from_last, 1, 0)
        filled = jnp.where(from_first | from_last, 1.0, 0.0).astype(jnp.bfloat16)
        slot_grad_ref[s] = blocks_ref[index] * filled
        for ref, out, axis in ((left_ref, left_out, 1), (right_ref, right_out, 0)):
            product = lax.dot_general(
                slot_grad_ref[s],
                slot_grad_ref[s],
                (((axis,), (axis,)), ((), ())),
                preferred_element_type=jnp.float32,
            )
            ref[s] = DECAY * ref[s] + (1.0 - DECAY) * product
            store = pltpu.make_async_copy(ref.at[s], out.at[s], stat_sem.at[len(stores)])
            store.start()
            stores.append(store)

    for copy in [left_swap, right_swap, block_swap]:
        copy.wait_send()
    for other in others:
        strip_copy(me, other).wait_send()
        sum_copy(me, other).wait_send()
    for store in stores:
        store.wait()
    for other in others:
        back_copy(other, me).wait_recv()
    for p in range(n):
        update_ref[p] = returned_ref[place_ref[p]]
    for other in others:
        back_copy(me, other).wait_send()


def exchange(n, grad_shards, offsets, owners, left_stats, right_stats, left_root, right_root):
    blocks, strip, size = grad_shards.shape
    capacity = left_root.shape[0]
    half = jnp.bfloat16
    anywhere = pl.BlockSpec(memory_space=pl.ANY)
    many = pltpu.SemaphoreType.DMA((n,))
    operands = [
        pltpu.with_memory_space_constraint(array, pltpu.HBM)
        for array in (
            offsets,
            owners,
            grad_shards,
            left_stats,
            right_stats,
            left_root,
            right_root,
        )
    ]
    return pl.pallas_call(
        functools.partial(exchange_kernel, n),
        out_shape=(
            jax.ShapeDtypeStruct((n, strip, size), half),
            jax.ShapeDtypeStruct(left_stats.shape, jnp.float32),
            jax.ShapeDtypeStruct(right_stats.shape, jnp.float32),
        ),
        in_specs=[anywhere] * len(operands),
        out_specs=(pl.BlockSpec(memory_space=pltpu.VMEM), anywhere, anywhere),
        scratch_shapes=[
            pltpu.SMEM((n,), jnp.int32),
            pltpu.SMEM((n,), jnp.int32),
            pltpu.SMEM((n,), jnp.int32),
            pltpu.SMEM((n,), jnp.int32),
            pltpu.VMEM((blocks, strip, size), half),
            pltpu.VMEM((n, strip, size), half),
            pltpu.VMEM((2, size, size), half),
            pltpu.VMEM((capacity, size, size), half),
            pltpu.VMEM((capacity, size, size), half),
            pltpu.VMEM((2, size, size), half),
            pltpu.VMEM((2, size, size), half),
            pltpu.VMEM((2, size, size), half),
            pltpu.VMEM((size, size), half),
            pltpu.VMEM((n, strip, size), half),
            pltpu.VMEM((capacity, size, size), half),
            pltpu.VMEM((capacity, size, size), jnp.float32),
            pltpu.VMEM((capacity, size, size), jnp.float32),
            pltpu.VMEM((n, 8, 128), jnp.float32),
            pltpu.SemaphoreType.DMA((len(operands),)),
            pltpu.SemaphoreType.DMA((2 * capacity,)),
            many,
            many,
            many,
            many,
            many,
            many,
            pltpu.SemaphoreType.DMA((3,)),
            pltpu.SemaphoreType.DMA((3,)),
        ],
        compiler_params=pltpu.CompilerParams(
            collective_id=0, has_side_effects=True, vmem_limit_bytes=32 * 1024 * 1024
        ),
        cost_estimate=pl.CostEstimate(
            flops=4 * (1 + capacity) * size**3,
            bytes_accessed=32 * 1024 * 1024,
            transcendentals=0,
        ),
        name="exchange",
    )(*operands)


def store_kernel(*refs):
    count = (len(refs) - 1) // 2
    sources, targets, sems = refs[:count], refs[count : 2 * count], refs[-1]
    copies = []
    for source, target in zip(sources, targets):
        pieces = 4
        size = source.shape[0] * source.shape[1] // pieces
        for piece in range(pieces):
            if source.shape[0] >= pieces:
                step = source.shape[0] // pieces
                part = pl.ds(piece * step, step)
                pair = (source.at[part], target.at[part])
            else:
                index, row = divmod(piece * size, source.shape[1])
                part = pl.ds(row, size)
                pair = (source.at[index, part], target.at[index, part])
            copy = pltpu.make_async_copy(*pair, sems.at[len(copies)])
            copy.start()
            copies.append(copy)
    for copy in copies:
        copy.wait()


def store(*arrays):
    anywhere = pl.BlockSpec(memory_space=pl.ANY)
    return pl.pallas_call(
        store_kernel,
        out_shape=tuple(jax.ShapeDtypeStruct(a.shape, a.dtype) for a in arrays),
        in_specs=[pl.BlockSpec(memory_space=pltpu.VMEM)] * len(arrays),
        out_specs=(anywhere,) * len(arrays),
        scratch_shapes=[pltpu.SemaphoreType.DMA((4 * len(arrays),))],
        compiler_params=pltpu.CompilerParams(vmem_limit_bytes=16 * 1024 * 1024),
        name="store",
    )(*arrays)


def body(grad_shards, offsets, owners, left_stats, right_stats, left_root, right_root):
    n = lax.axis_size(AXIS)
    blocks, strip, _ = grad_shards.shape
    if blocks != n or strip % 16 or left_stats.shape[0] != 2:
        return padded_body(
            grad_shards, offsets, owners, left_stats, right_stats, left_root, right_root
        )
    return store(
        *exchange(
            n, grad_shards, offsets, owners, left_stats, right_stats, left_root, right_root
        )
    )


def solution(mesh):
    placed = (
        P("groups", "fsdp", None),
        P("groups"),
        P("groups"),
        P(("groups", "fsdp"), None, None),
        P(("groups", "fsdp"), None, None),
        P(("groups", "fsdp"), None, None),
        P(("groups", "fsdp"), None, None),
    )
    return jax.shard_map(
        body,
        mesh=mesh,
        in_specs=placed,
        out_specs=(
            P("groups", "fsdp", None),
            P(("groups", "fsdp"), None, None),
            P(("groups", "fsdp"), None, None),
        ),
        check_vma=False,
    )
```

```python
import functools

import jax
import jax.numpy as jnp
from jax import lax
from jax.experimental import pallas as pl
from jax.experimental.pallas import tpu as pltpu
from jax.sharding import PartitionSpec as P

DECAY = 0.999
CLIP_RMS = 1.0
EPSILON = 1e-06


def slot_tables(owners, peer_count, capacity):
    block_count = owners.shape[0]
    block_ids = jnp.arange(block_count, dtype=jnp.int32)
    same_owner = owners[None, :] == owners[:, None]
    earlier = block_ids[None, :] < block_ids[:, None]
    slot_rank = jnp.sum((same_owner & earlier).astype(jnp.int32), axis=1)
    slot_ids = jnp.arange(capacity, dtype=jnp.int32)
    holder_ids = jnp.arange(peer_count, dtype=jnp.int32)
    slot_match = (owners[None, None, :] == holder_ids[None, :, None]) & (
        slot_rank[None, None, :] == slot_ids[:, None, None]
    )
    return (slot_rank, slot_match)


def precondition(gradient, grad_mean, left_old, right_old, left_inv, right_inv, clip_factor):
    left_new = DECAY * left_old + (1.0 - DECAY) * jnp.dot(
        gradient, gradient.T, preferred_element_type=jnp.float32
    )
    right_new = DECAY * right_old + (1.0 - DECAY) * jnp.dot(
        gradient.T, gradient, preferred_element_type=jnp.float32
    )
    left_half = jnp.dot(left_inv, gradient, preferred_element_type=jnp.float32).astype(jnp.bfloat16)
    direction = jnp.dot(left_half, right_inv, preferred_element_type=jnp.float32)
    graft_scale = jnp.sqrt(grad_mean / (jnp.mean(direction * direction) + EPSILON))
    return (left_new, right_new, (clip_factor * (graft_scale * direction)).astype(jnp.bfloat16))


def padded_body(grad_shards, offsets, owners, left_stats, right_stats, left_root, right_root):
    peer_count = lax.axis_size("fsdp")
    capacity = left_stats.shape[0]
    block_count, strip_rows, block_size = grad_shards.shape
    slot_rank, slot_match = slot_tables(owners, peer_count, capacity)
    positions = jnp.arange(block_count, dtype=jnp.int32)
    at_position = (offsets[None, :] == positions[:, None]).astype(jnp.int32)
    matched = slot_match.astype(jnp.int32)
    source_rows = jnp.sum(matched * offsets[None, None, :], axis=2).reshape(-1)
    occupied = jnp.sum(matched, axis=2).reshape(-1)
    picked = jnp.take(grad_shards, source_rows, axis=0)
    picked = jnp.where(occupied[:, None, None] > 0, picked, jnp.zeros_like(picked))
    outgoing = picked.reshape(capacity, peer_count * strip_rows, block_size)
    arrived = lax.all_to_all(outgoing, "fsdp", split_axis=1, concat_axis=1, tiled=True)
    widened = arrived.astype(jnp.float32)
    slot_squares = jnp.sum(widened * widened, axis=(1, 2))
    entries = block_count * block_size * block_size
    local_grad = grad_shards.astype(jnp.float32)
    square_sum = lax.psum(jnp.sum(local_grad * local_grad), "fsdp")
    clip_factor = jnp.minimum(1.0, CLIP_RMS * lax.rsqrt(square_sum / entries))
    left_list = []
    right_list = []
    update_list = []
    for slot_index in range(capacity):
        grad_mean = slot_squares[slot_index] / (block_size * block_size)
        left_new, right_new, slot_update = precondition(
            arrived[slot_index],
            grad_mean,
            left_stats[slot_index],
            right_stats[slot_index],
            left_root[slot_index],
            right_root[slot_index],
            clip_factor,
        )
        left_list.append(left_new)
        right_list.append(right_new)
        update_list.append(slot_update)
    slot_updates = jnp.stack(update_list)
    returned = lax.all_to_all(slot_updates, "fsdp", split_axis=1, concat_axis=1, tiled=True)
    anchor = slot_rank * peer_count + owners
    where_from = jnp.sum(at_position * anchor[None, :], axis=1)
    update = jnp.take(
        returned.reshape(capacity * peer_count, strip_rows, block_size), where_from, axis=0
    )
    return (update, jnp.stack(left_list), jnp.stack(right_list))


AXIS = "fsdp"
MESH = pl.DeviceIdType.MESH


def mean_square(values):
    return jnp.sum(values * values, axis=(0, 1), keepdims=True) / values.size


def exchange_kernel(
    n,
    offsets_hbm,
    owners_hbm,
    grad_hbm,
    left_hbm,
    right_hbm,
    left_root_hbm,
    right_root_hbm,
    update_ref,
    left_out,
    right_out,
    offsets_ref,
    owners_ref,
    table_ref,
    place_ref,
    grad_ref,
    outgoing_ref,
    blocks_ref,
    left_root_ref,
    right_root_ref,
    root_out_ref,
    root_in_ref,
    root_ref,
    slot_update_ref,
    returned_ref,
    left_ref,
    right_ref,
    sums_ref,
    local_sem,
    stat_sem,
    strip_send,
    strip_recv,
    sum_send,
    sum_recv,
    back_send,
    back_recv,
    pair_send,
    pair_recv,
):
    strip, block_size = grad_ref.shape[1:]
    capacity = left_root_hbm.shape[0]
    pair_count = n // 2
    me = lax.axis_index(AXIS)
    pair = me // 2
    side = me - 2 * pair
    sibling = me + 1 - 2 * side

    def wrapped(k):
        ahead = pair + k
        return jnp.where(ahead >= pair_count, ahead - pair_count, ahead)

    middle = pair_count // 2
    steps = sorted(range(1, pair_count), key=lambda k: k)
    to_first = [2 * wrapped(k) for k in steps]
    to_last = [2 * wrapped(k) + 1 for k in steps]
    others = to_first + to_last + [sibling]

    def rows_of(device):
        return pl.ds(pl.multiple_of(device * strip, strip), strip)

    def remote(source, target, send_sem, recv_sem, device):
        return pltpu.make_async_remote_copy(
            src_ref=source,
            dst_ref=target,
            send_sem=send_sem,
            recv_sem=recv_sem,
            device_id={AXIS: device},
            device_id_type=MESH,
        )

    def strip_copy(source, target):
        return remote(
            outgoing_ref.at[target],
            blocks_ref.at[target - 2 * (target // 2), rows_of(source)],
            strip_send.at[target],
            strip_recv.at[source],
            target,
        )

    def sum_copy(source, target):
        row = sums_ref.at[source]
        return remote(row, row, sum_send.at[target], sum_recv.at[source], target)

    def back_copy(source, target):
        return remote(
            slot_update_ref.at[rows_of(target)],
            returned_ref.at[source],
            back_send.at[target],
            back_recv.at[source],
            target,
        )

    def pair_copy(index, source, target):
        return remote(source, target, pair_send.at[index], pair_recv.at[index], sibling)

    barrier = pltpu.get_barrier_semaphore()
    for other in others:
        pl.semaphore_signal(barrier, inc=1, device_id={AXIS: other}, device_id_type=MESH)
    loads = [
        pltpu.make_async_copy(source, target, local_sem.at[i])
        for i, (source, target) in enumerate(
            [
                (offsets_hbm, offsets_ref),
                (owners_hbm, owners_ref),
                (grad_hbm, grad_ref),
                (left_root_hbm, left_root_ref),
                (right_root_hbm, right_root_ref),
                (left_hbm, left_ref),
                (right_hbm, right_ref),
            ]
        )
    ]
    for load in loads[:5]:
        load.start()

    loads[0].wait()
    loads[1].wait()
    owners = [owners_ref[b] for b in range(n)]
    offsets = [offsets_ref[b] for b in range(n)]
    pairs = [owner >> 1 for owner in owners]
    for k in range(pair_count):
        first = offsets[0]
        last = offsets[0]
        for b in range(1, n):
            last = jnp.where(pairs[b] == k, offsets[b], last)
        for b in range(n - 1, -1, -1):
            first = jnp.where(pairs[b] == k, offsets[b], first)
        table_ref[2 * k] = first
        table_ref[2 * k + 1] = last
    first_owner = owners[0]
    last_owner = owners[0]
    for b in range(1, n):
        last_owner = jnp.where(pairs[b] == pair, owners[b], last_owner)
    for b in range(n - 1, -1, -1):
        first_owner = jnp.where(pairs[b] == pair, owners[b], first_owner)
    first_side = first_owner & 1
    last_side = last_owner & 1
    last_rank = jnp.where(first_owner == last_owner, 1, 0)
    my_side = jnp.where(side == 0, first_side, last_side)
    my_rank = jnp.where(side == 0, 0, last_rank)
    sibling_rank = jnp.where(side == 0, last_rank, 0)
    own_root = my_side == side

    loads[2].wait()
    pl.semaphore_wait(barrier, n - 1)

    def send_strip(other):
        outgoing_ref[other] = grad_ref[table_ref[other]]
        strip_copy(me, other).start()

    for other in to_first:
        send_strip(other)
    squares = jnp.zeros((strip, block_size), jnp.float32)
    for b in range(n):
        wide = grad_ref[b].astype(jnp.float32)
        squares += wide * wide
    partial = squares[0:8]
    for r in range(8, strip, 8):
        partial += squares[r : r + 8]
    lanes = partial[:, 0:128]
    for c in range(128, block_size, 128):
        lanes += partial[:, c : c + 128]
    sums_ref[me] = lanes
    for other in others:
        sum_copy(me, other).start()
    send_strip(sibling)
    for other in to_last:
        send_strip(other)
    blocks_ref[side, rows_of(me)] = grad_ref[table_ref[me]]

    loads[3].wait()
    root_out_ref[0] = left_root_ref[sibling_rank]
    left_swap = pair_copy(0, root_out_ref.at[0], root_in_ref.at[0])
    left_swap.start()
    loads[4].wait()
    root_out_ref[1] = right_root_ref[sibling_rank]
    right_swap = pair_copy(1, root_out_ref.at[1], root_in_ref.at[1])
    right_swap.start()
    loads[5].start()
    loads[6].start()

    for other in others:
        sum_copy(other, me).wait_recv()
    total = jnp.sum(jnp.sum(sums_ref[...], axis=0), axis=(0, 1), keepdims=True)
    clip_factor = jnp.minimum(1.0, CLIP_RMS * lax.rsqrt(total / (n * block_size * block_size)))
    left_swap.wait_recv()
    right_swap.wait_recv()
    root_ref[0] = jnp.where(own_root, left_root_ref[my_rank], root_in_ref[0])
    root_ref[1] = jnp.where(own_root, right_root_ref[my_rank], root_in_ref[1])

    swapped = pair_copy(2, blocks_ref.at[1 - side], blocks_ref.at[1 - side])
    stats = ((left_ref, left_out, 1), (right_ref, right_out, 0))
    stores = []

    def product(index, axis):
        return (1.0 - DECAY) * lax.dot_general(
            blocks_ref[index],
            blocks_ref[index],
            (((axis,), (axis,)), ((), ())),
            preferred_element_type=jnp.float32,
        )

    def add_first():
        loads[5].wait()
        loads[6].wait()
        for ref, _, axis in stats:
            ref[0] = DECAY * ref[0] + jnp.where(first_side == side, product(0, axis), 0.0)

    def add_last():
        for ref, out, axis in stats:
            change = product(1, axis)
            for s in range(capacity):
                old = ref[s] if s == 0 else DECAY * ref[s]
                here = (last_side == side) & (last_rank == s)
                ref[s] = old + jnp.where(here, change, 0.0)
                store = pltpu.make_async_copy(ref.at[s], out.at[s], stat_sem.at[len(stores)])
                store.start()
                stores.append(store)

    @pl.when(side == 1)
    def _():
        swapped.wait_recv()
        add_first()

    half = n // 2
    near = me // half
    far = 1 - near

    def partial_half(part):
        span = pl.ds(pl.multiple_of(part * (block_size // 2), block_size // 2), block_size // 2)
        rows = blocks_ref[side, span]
        wide = rows.astype(jnp.float32)
        squares = jnp.sum(wide * wide, axis=(0, 1), keepdims=True)
        product = jnp.dot(root_ref[0, :, span], rows, preferred_element_type=jnp.float32)
        return squares, product

    offset = me - near * half
    for k in range(1, half):
        ahead = offset + k
        ahead = jnp.where(ahead >= half, ahead - half, ahead)
        strip_copy(near * half + ahead, me).wait_recv()
    near_squares, near_product = partial_half(near)
    for k in range(half):
        strip_copy(far * half + k, me).wait_recv()
    block_swap = pair_copy(2, blocks_ref.at[side], blocks_ref.at[side])
    block_swap.start()

    far_squares, far_product = partial_half(far)
    grad_mean = (near_squares + far_squares) / (block_size * block_size)
    left_half = near_product + far_product
    direction = jnp.dot(
        left_half.astype(jnp.bfloat16),
        root_ref[1],
        preferred_element_type=jnp.float32,
    )
    graft_scale = jnp.sqrt(grad_mean / (mean_square(direction) + EPSILON))
    slot_update_ref[...] = (clip_factor * (graft_scale * direction)).astype(jnp.bfloat16)
    for a, b in zip(to_first, to_last):
        back_copy(me, a).start()
        back_copy(me, b).start()
    back_copy(me, sibling).start()
    returned_ref[me] = slot_update_ref[rows_of(me)]

    for p in range(n):
        holder = 0
        for d in range(n):
            holder = jnp.where(table_ref[d] == p, d, holder)
        place_ref[p] = holder

    @pl.when(side == 0)
    def _():
        add_first()
        swapped.wait_recv()

    add_last()
    for copy in [left_swap, right_swap, block_swap]:
        copy.wait_send()
    for other in others:
        strip_copy(me, other).wait_send()
        sum_copy(me, other).wait_send()
    for copy in stores:
        copy.wait()
    for other in others:
        back_copy(other, me).wait_recv()
    for p in range(n):
        update_ref[p] = returned_ref[place_ref[p]]
    for other in others:
        back_copy(me, other).wait_send()


def exchange(n, grad_shards, offsets, owners, left_stats, right_stats, left_root, right_root):
    blocks, strip, size = grad_shards.shape
    capacity = left_root.shape[0]
    half = jnp.bfloat16
    anywhere = pl.BlockSpec(memory_space=pl.ANY)
    many = pltpu.SemaphoreType.DMA((n,))
    operands = [
        pltpu.with_memory_space_constraint(array, pltpu.HBM)
        for array in (
            offsets,
            owners,
            grad_shards,
            left_stats,
            right_stats,
            left_root,
            right_root,
        )
    ]
    return pl.pallas_call(
        functools.partial(exchange_kernel, n),
        out_shape=(
            jax.ShapeDtypeStruct((n, strip, size), half),
            jax.ShapeDtypeStruct(left_stats.shape, jnp.float32),
            jax.ShapeDtypeStruct(right_stats.shape, jnp.float32),
        ),
        in_specs=[anywhere] * len(operands),
        out_specs=(pl.BlockSpec(memory_space=pltpu.VMEM), anywhere, anywhere),
        scratch_shapes=[
            pltpu.SMEM((n,), jnp.int32),
            pltpu.SMEM((n,), jnp.int32),
            pltpu.SMEM((n,), jnp.int32),
            pltpu.SMEM((n,), jnp.int32),
            pltpu.VMEM((blocks, strip, size), half),
            pltpu.VMEM((n, strip, size), half),
            pltpu.VMEM((2, size, size), half),
            pltpu.VMEM((capacity, size, size), half),
            pltpu.VMEM((capacity, size, size), half),
            pltpu.VMEM((2, size, size), half),
            pltpu.VMEM((2, size, size), half),
            pltpu.VMEM((2, size, size), half),
            pltpu.VMEM((size, size), half),
            pltpu.VMEM((n, strip, size), half),
            pltpu.VMEM((capacity, size, size), jnp.float32),
            pltpu.VMEM((capacity, size, size), jnp.float32),
            pltpu.VMEM((n, 8, 128), jnp.float32),
            pltpu.SemaphoreType.DMA((len(operands),)),
            pltpu.SemaphoreType.DMA((2 * capacity,)),
            many,
            many,
            many,
            many,
            many,
            many,
            pltpu.SemaphoreType.DMA((3,)),
            pltpu.SemaphoreType.DMA((3,)),
        ],
        compiler_params=pltpu.CompilerParams(
            collective_id=0, has_side_effects=True, vmem_limit_bytes=32 * 1024 * 1024
        ),
        cost_estimate=pl.CostEstimate(
            flops=4 * (1 + capacity) * size**3,
            bytes_accessed=32 * 1024 * 1024,
            transcendentals=0,
        ),
        name="exchange",
    )(*operands)


def store_kernel(*refs):
    count = (len(refs) - 1) // 2
    sources, targets, sems = refs[:count], refs[count : 2 * count], refs[-1]
    copies = []
    for source, target in zip(sources, targets):
        pieces = 4
        size = source.shape[0] * source.shape[1] // pieces
        for piece in range(pieces):
            if source.shape[0] >= pieces:
                step = source.shape[0] // pieces
                part = pl.ds(piece * step, step)
                pair = (source.at[part], target.at[part])
            else:
                index, row = divmod(piece * size, source.shape[1])
                part = pl.ds(row, size)
                pair = (source.at[index, part], target.at[index, part])
            copy = pltpu.make_async_copy(*pair, sems.at[len(copies)])
            copy.start()
            copies.append(copy)
    for copy in copies:
        copy.wait()


def store(*arrays):
    anywhere = pl.BlockSpec(memory_space=pl.ANY)
    return pl.pallas_call(
        store_kernel,
        out_shape=tuple(jax.ShapeDtypeStruct(a.shape, a.dtype) for a in arrays),
        in_specs=[pl.BlockSpec(memory_space=pltpu.VMEM)] * len(arrays),
        out_specs=(anywhere,) * len(arrays),
        scratch_shapes=[pltpu.SemaphoreType.DMA((4 * len(arrays),))],
        compiler_params=pltpu.CompilerParams(vmem_limit_bytes=16 * 1024 * 1024),
        name="store",
    )(*arrays)


def body(grad_shards, offsets, owners, left_stats, right_stats, left_root, right_root):
    n = lax.axis_size(AXIS)
    blocks, strip, _ = grad_shards.shape
    if blocks != n or strip % 16 or left_stats.shape[0] != 2:
        return padded_body(
            grad_shards, offsets, owners, left_stats, right_stats, left_root, right_root
        )
    return store(
        *exchange(
            n, grad_shards, offsets, owners, left_stats, right_stats, left_root, right_root
        )
    )


def solution(mesh):
    placed = (
        P("groups", "fsdp", None),
        P("groups"),
        P("groups"),
        P(("groups", "fsdp"), None, None),
        P(("groups", "fsdp"), None, None),
        P(("groups", "fsdp"), None, None),
        P(("groups", "fsdp"), None, None),
    )
    return jax.shard_map(
        body,
        mesh=mesh,
        in_specs=placed,
        out_specs=(
            P("groups", "fsdp", None),
            P(("groups", "fsdp"), None, None),
            P(("groups", "fsdp"), None, None),
        ),
        check_vma=False,
    )
```

```python
import functools

import jax
import jax.numpy as jnp
from jax import lax
from jax.experimental import pallas as pl
from jax.experimental.pallas import tpu as pltpu
from jax.sharding import PartitionSpec as P

DECAY = 0.999
CLIP_RMS = 1.0
EPSILON = 1e-06


def slot_tables(owners, peer_count, capacity):
    block_count = owners.shape[0]
    block_ids = jnp.arange(block_count, dtype=jnp.int32)
    same_owner = owners[None, :] == owners[:, None]
    earlier = block_ids[None, :] < block_ids[:, None]
    slot_rank = jnp.sum((same_owner & earlier).astype(jnp.int32), axis=1)
    slot_ids = jnp.arange(capacity, dtype=jnp.int32)
    holder_ids = jnp.arange(peer_count, dtype=jnp.int32)
    slot_match = (owners[None, None, :] == holder_ids[None, :, None]) & (
        slot_rank[None, None, :] == slot_ids[:, None, None]
    )
    return (slot_rank, slot_match)


def precondition(gradient, grad_mean, left_old, right_old, left_inv, right_inv, clip_factor):
    left_new = DECAY * left_old + (1.0 - DECAY) * jnp.dot(
        gradient, gradient.T, preferred_element_type=jnp.float32
    )
    right_new = DECAY * right_old + (1.0 - DECAY) * jnp.dot(
        gradient.T, gradient, preferred_element_type=jnp.float32
    )
    left_half = jnp.dot(left_inv, gradient, preferred_element_type=jnp.float32).astype(jnp.bfloat16)
    direction = jnp.dot(left_half, right_inv, preferred_element_type=jnp.float32)
    graft_scale = jnp.sqrt(grad_mean / (jnp.mean(direction * direction) + EPSILON))
    return (left_new, right_new, (clip_factor * (graft_scale * direction)).astype(jnp.bfloat16))


def padded_body(grad_shards, offsets, owners, left_stats, right_stats, left_root, right_root):
    peer_count = lax.axis_size("fsdp")
    capacity = left_stats.shape[0]
    block_count, strip_rows, block_size = grad_shards.shape
    slot_rank, slot_match = slot_tables(owners, peer_count, capacity)
    positions = jnp.arange(block_count, dtype=jnp.int32)
    at_position = (offsets[None, :] == positions[:, None]).astype(jnp.int32)
    matched = slot_match.astype(jnp.int32)
    source_rows = jnp.sum(matched * offsets[None, None, :], axis=2).reshape(-1)
    occupied = jnp.sum(matched, axis=2).reshape(-1)
    picked = jnp.take(grad_shards, source_rows, axis=0)
    picked = jnp.where(occupied[:, None, None] > 0, picked, jnp.zeros_like(picked))
    outgoing = picked.reshape(capacity, peer_count * strip_rows, block_size)
    arrived = lax.all_to_all(outgoing, "fsdp", split_axis=1, concat_axis=1, tiled=True)
    widened = arrived.astype(jnp.float32)
    slot_squares = jnp.sum(widened * widened, axis=(1, 2))
    entries = block_count * block_size * block_size
    local_grad = grad_shards.astype(jnp.float32)
    square_sum = lax.psum(jnp.sum(local_grad * local_grad), "fsdp")
    clip_factor = jnp.minimum(1.0, CLIP_RMS * lax.rsqrt(square_sum / entries))
    left_list = []
    right_list = []
    update_list = []
    for slot_index in range(capacity):
        grad_mean = slot_squares[slot_index] / (block_size * block_size)
        left_new, right_new, slot_update = precondition(
            arrived[slot_index],
            grad_mean,
            left_stats[slot_index],
            right_stats[slot_index],
            left_root[slot_index],
            right_root[slot_index],
            clip_factor,
        )
        left_list.append(left_new)
        right_list.append(right_new)
        update_list.append(slot_update)
    slot_updates = jnp.stack(update_list)
    returned = lax.all_to_all(slot_updates, "fsdp", split_axis=1, concat_axis=1, tiled=True)
    anchor = slot_rank * peer_count + owners
    where_from = jnp.sum(at_position * anchor[None, :], axis=1)
    update = jnp.take(
        returned.reshape(capacity * peer_count, strip_rows, block_size), where_from, axis=0
    )
    return (update, jnp.stack(left_list), jnp.stack(right_list))


AXIS = "fsdp"
MESH = pl.DeviceIdType.MESH


def mean_square(values):
    return jnp.sum(values * values, axis=(0, 1), keepdims=True) / values.size


def exchange_kernel(
    n,
    offsets_hbm,
    owners_hbm,
    grad_hbm,
    left_hbm,
    right_hbm,
    left_root_hbm,
    right_root_hbm,
    update_ref,
    left_out,
    right_out,
    offsets_ref,
    owners_ref,
    table_ref,
    place_ref,
    grad_ref,
    outgoing_ref,
    blocks_ref,
    left_root_ref,
    right_root_ref,
    root_out_ref,
    root_in_ref,
    root_ref,
    slot_update_ref,
    returned_ref,
    left_ref,
    right_ref,
    sums_ref,
    local_sem,
    stat_sem,
    strip_send,
    strip_recv,
    sum_send,
    sum_recv,
    back_send,
    back_recv,
    pair_send,
    pair_recv,
):
    strip, block_size = grad_ref.shape[1:]
    capacity = left_root_hbm.shape[0]
    pair_count = n // 2
    me = lax.axis_index(AXIS)
    pair = me // 2
    side = me - 2 * pair
    sibling = me + 1 - 2 * side

    def wrapped(k):
        ahead = pair + k
        return jnp.where(ahead >= pair_count, ahead - pair_count, ahead)

    middle = pair_count // 2
    steps = sorted(range(1, pair_count), key=lambda k: k)
    to_first = [2 * wrapped(k) for k in steps]
    to_last = [2 * wrapped(k) + 1 for k in steps]
    others = to_first + to_last + [sibling]

    def rows_of(device):
        return pl.ds(pl.multiple_of(device * strip, strip), strip)

    def remote(source, target, send_sem, recv_sem, device):
        return pltpu.make_async_remote_copy(
            src_ref=source,
            dst_ref=target,
            send_sem=send_sem,
            recv_sem=recv_sem,
            device_id={AXIS: device},
            device_id_type=MESH,
        )

    def strip_copy(source, target):
        return remote(
            outgoing_ref.at[target],
            blocks_ref.at[target - 2 * (target // 2), rows_of(source)],
            strip_send.at[target],
            strip_recv.at[source],
            target,
        )

    def sum_copy(source, target):
        row = sums_ref.at[source]
        return remote(row, row, sum_send.at[target], sum_recv.at[source], target)

    def back_copy(source, target):
        return remote(
            slot_update_ref.at[rows_of(target)],
            returned_ref.at[source],
            back_send.at[target],
            back_recv.at[source],
            target,
        )

    def pair_copy(index, source, target):
        return remote(source, target, pair_send.at[index], pair_recv.at[index], sibling)

    barrier = pltpu.get_barrier_semaphore()
    loads = [
        pltpu.make_async_copy(source, target, local_sem.at[i])
        for i, (source, target) in enumerate(
            [
                (offsets_hbm, offsets_ref),
                (owners_hbm, owners_ref),
                (grad_hbm, grad_ref),
                (left_root_hbm, left_root_ref),
                (right_root_hbm, right_root_ref),
                (left_hbm, left_ref),
                (right_hbm, right_ref),
            ]
        )
    ]
    for load in loads[:3]:
        load.start()
    for other in others:
        pl.semaphore_signal(barrier, inc=1, device_id={AXIS: other}, device_id_type=MESH)
    for load in loads[3:5]:
        load.start()

    loads[0].wait()
    loads[1].wait()
    owners = [owners_ref[b] for b in range(n)]
    offsets = [offsets_ref[b] for b in range(n)]
    pairs = [owner >> 1 for owner in owners]
    for k in range(pair_count):
        first = offsets[0]
        last = offsets[0]
        for b in range(1, n):
            last = jnp.where(pairs[b] == k, offsets[b], last)
        for b in range(n - 1, -1, -1):
            first = jnp.where(pairs[b] == k, offsets[b], first)
        table_ref[2 * k] = first
        table_ref[2 * k + 1] = last
    first_owner = owners[0]
    last_owner = owners[0]
    for b in range(1, n):
        last_owner = jnp.where(pairs[b] == pair, owners[b], last_owner)
    for b in range(n - 1, -1, -1):
        first_owner = jnp.where(pairs[b] == pair, owners[b], first_owner)
    first_side = first_owner & 1
    last_side = last_owner & 1
    last_rank = jnp.where(first_owner == last_owner, 1, 0)
    my_side = jnp.where(side == 0, first_side, last_side)
    my_rank = jnp.where(side == 0, 0, last_rank)
    sibling_rank = jnp.where(side == 0, last_rank, 0)
    own_root = my_side == side

    loads[2].wait()
    pl.semaphore_wait(barrier, n - 1)

    def send_strip(other):
        outgoing_ref[other] = grad_ref[table_ref[other]]
        strip_copy(me, other).start()

    for other in to_first:
        send_strip(other)
    squares = jnp.zeros((strip, block_size), jnp.float32)
    for b in range(n):
        wide = grad_ref[b].astype(jnp.float32)
        squares += wide * wide
    partial = squares[0:8]
    for r in range(8, strip, 8):
        partial += squares[r : r + 8]
    lanes = partial[:, 0:128]
    for c in range(128, block_size, 128):
        lanes += partial[:, c : c + 128]
    sums_ref[me] = lanes
    for other in others:
        sum_copy(me, other).start()
    send_strip(sibling)
    for other in to_last:
        send_strip(other)
    blocks_ref[side, rows_of(me)] = grad_ref[table_ref[me]]

    loads[3].wait()
    root_out_ref[0] = left_root_ref[sibling_rank]
    left_swap = pair_copy(0, root_out_ref.at[0], root_in_ref.at[0])
    left_swap.start()
    loads[4].wait()
    root_out_ref[1] = right_root_ref[sibling_rank]
    right_swap = pair_copy(1, root_out_ref.at[1], root_in_ref.at[1])
    right_swap.start()
    loads[5].start()
    loads[6].start()

    for other in others:
        sum_copy(other, me).wait_recv()
    total = jnp.sum(jnp.sum(sums_ref[...], axis=0), axis=(0, 1), keepdims=True)
    clip_factor = jnp.minimum(1.0, CLIP_RMS * lax.rsqrt(total / (n * block_size * block_size)))
    left_swap.wait_recv()
    right_swap.wait_recv()
    root_ref[0] = jnp.where(own_root, left_root_ref[my_rank], root_in_ref[0])
    root_ref[1] = jnp.where(own_root, right_root_ref[my_rank], root_in_ref[1])

    swapped = pair_copy(2, blocks_ref.at[1 - side], blocks_ref.at[1 - side])
    stats = ((left_ref, left_out, 1), (right_ref, right_out, 0))
    stores = []

    def product(index, axis):
        return (1.0 - DECAY) * lax.dot_general(
            blocks_ref[index],
            blocks_ref[index],
            (((axis,), (axis,)), ((), ())),
            preferred_element_type=jnp.float32,
        )

    def add_first():
        loads[5].wait()
        loads[6].wait()
        for ref, _, axis in stats:
            ref[0] = DECAY * ref[0] + jnp.where(first_side == side, product(0, axis), 0.0)

    def add_last():
        for ref, out, axis in stats:
            change = product(1, axis)
            for s in range(capacity):
                old = ref[s] if s == 0 else DECAY * ref[s]
                here = (last_side == side) & (last_rank == s)
                ref[s] = old + jnp.where(here, change, 0.0)
                store = pltpu.make_async_copy(ref.at[s], out.at[s], stat_sem.at[len(stores)])
                store.start()
                stores.append(store)

    @pl.when(side == 1)
    def _():
        swapped.wait_recv()
        add_first()

    half = n // 2
    near = me // half
    far = 1 - near

    def partial_half(part):
        span = pl.ds(pl.multiple_of(part * (block_size // 2), block_size // 2), block_size // 2)
        rows = blocks_ref[side, span]
        wide = rows.astype(jnp.float32)
        squares = jnp.sum(wide * wide, axis=(0, 1), keepdims=True)
        product = jnp.dot(root_ref[0, :, span], rows, preferred_element_type=jnp.float32)
        return squares, product

    offset = me - near * half
    for k in range(1, half):
        ahead = offset + k
        ahead = jnp.where(ahead >= half, ahead - half, ahead)
        strip_copy(near * half + ahead, me).wait_recv()
    near_squares, near_product = partial_half(near)
    for k in range(half):
        strip_copy(far * half + k, me).wait_recv()
    block_swap = pair_copy(2, blocks_ref.at[side], blocks_ref.at[side])
    block_swap.start()

    far_squares, far_product = partial_half(far)
    grad_mean = (near_squares + far_squares) / (block_size * block_size)
    left_half = near_product + far_product
    direction = jnp.dot(
        left_half.astype(jnp.bfloat16),
        root_ref[1],
        preferred_element_type=jnp.float32,
    )
    graft_scale = jnp.sqrt(grad_mean / (mean_square(direction) + EPSILON))
    slot_update_ref[...] = (clip_factor * (graft_scale * direction)).astype(jnp.bfloat16)
    for a, b in zip(to_first, to_last):
        back_copy(me, a).start()
        back_copy(me, b).start()
    back_copy(me, sibling).start()
    returned_ref[me] = slot_update_ref[rows_of(me)]

    for p in range(n):
        holder = 0
        for d in range(n):
            holder = jnp.where(table_ref[d] == p, d, holder)
        place_ref[p] = holder

    @pl.when(side == 0)
    def _():
        add_first()
        swapped.wait_recv()

    add_last()
    for copy in [left_swap, right_swap, block_swap]:
        copy.wait_send()
    for other in others:
        strip_copy(me, other).wait_send()
        sum_copy(me, other).wait_send()
    for copy in stores:
        copy.wait()
    for other in others:
        back_copy(other, me).wait_recv()
    for p in range(n):
        update_ref[p] = returned_ref[place_ref[p]]
    for other in others:
        back_copy(me, other).wait_send()


def exchange(n, grad_shards, offsets, owners, left_stats, right_stats, left_root, right_root):
    blocks, strip, size = grad_shards.shape
    capacity = left_root.shape[0]
    half = jnp.bfloat16
    anywhere = pl.BlockSpec(memory_space=pl.ANY)
    many = pltpu.SemaphoreType.DMA((n,))
    operands = [
        pltpu.with_memory_space_constraint(array, pltpu.HBM)
        for array in (
            offsets,
            owners,
            grad_shards,
            left_stats,
            right_stats,
            left_root,
            right_root,
        )
    ]
    return pl.pallas_call(
        functools.partial(exchange_kernel, n),
        out_shape=(
            jax.ShapeDtypeStruct((n, strip, size), half),
            jax.ShapeDtypeStruct(left_stats.shape, jnp.float32),
            jax.ShapeDtypeStruct(right_stats.shape, jnp.float32),
        ),
        in_specs=[anywhere] * len(operands),
        out_specs=(pl.BlockSpec(memory_space=pltpu.VMEM), anywhere, anywhere),
        scratch_shapes=[
            pltpu.SMEM((n,), jnp.int32),
            pltpu.SMEM((n,), jnp.int32),
            pltpu.SMEM((n,), jnp.int32),
            pltpu.SMEM((n,), jnp.int32),
            pltpu.VMEM((blocks, strip, size), half),
            pltpu.VMEM((n, strip, size), half),
            pltpu.VMEM((2, size, size), half),
            pltpu.VMEM((capacity, size, size), half),
            pltpu.VMEM((capacity, size, size), half),
            pltpu.VMEM((2, size, size), half),
            pltpu.VMEM((2, size, size), half),
            pltpu.VMEM((2, size, size), half),
            pltpu.VMEM((size, size), half),
            pltpu.VMEM((n, strip, size), half),
            pltpu.VMEM((capacity, size, size), jnp.float32),
            pltpu.VMEM((capacity, size, size), jnp.float32),
            pltpu.VMEM((n, 8, 128), jnp.float32),
            pltpu.SemaphoreType.DMA((len(operands),)),
            pltpu.SemaphoreType.DMA((2 * capacity,)),
            many,
            many,
            many,
            many,
            many,
            many,
            pltpu.SemaphoreType.DMA((3,)),
            pltpu.SemaphoreType.DMA((3,)),
        ],
        compiler_params=pltpu.CompilerParams(
            collective_id=0, has_side_effects=True, vmem_limit_bytes=32 * 1024 * 1024
        ),
        cost_estimate=pl.CostEstimate(
            flops=4 * (1 + capacity) * size**3,
            bytes_accessed=32 * 1024 * 1024,
            transcendentals=0,
        ),
        name="exchange",
    )(*operands)


def store_kernel(*refs):
    count = (len(refs) - 1) // 2
    sources, targets, sems = refs[:count], refs[count : 2 * count], refs[-1]
    copies = []
    for source, target in zip(sources, targets):
        pieces = 2
        size = source.shape[0] * source.shape[1] // pieces
        for piece in range(pieces):
            if source.shape[0] >= pieces:
                step = source.shape[0] // pieces
                part = pl.ds(piece * step, step)
                pair = (source.at[part], target.at[part])
            else:
                index, row = divmod(piece * size, source.shape[1])
                part = pl.ds(row, size)
                pair = (source.at[index, part], target.at[index, part])
            copy = pltpu.make_async_copy(*pair, sems.at[len(copies)])
            copy.start()
            copies.append(copy)
    for copy in copies:
        copy.wait()


def store(*arrays):
    anywhere = pl.BlockSpec(memory_space=pl.ANY)
    return pl.pallas_call(
        store_kernel,
        out_shape=tuple(jax.ShapeDtypeStruct(a.shape, a.dtype) for a in arrays),
        in_specs=[pl.BlockSpec(memory_space=pltpu.VMEM)] * len(arrays),
        out_specs=(anywhere,) * len(arrays),
        scratch_shapes=[pltpu.SemaphoreType.DMA((2 * len(arrays),))],
        compiler_params=pltpu.CompilerParams(vmem_limit_bytes=16 * 1024 * 1024),
        name="store",
    )(*arrays)


def body(grad_shards, offsets, owners, left_stats, right_stats, left_root, right_root):
    n = lax.axis_size(AXIS)
    blocks, strip, _ = grad_shards.shape
    if blocks != n or strip % 16 or left_stats.shape[0] != 2:
        return padded_body(
            grad_shards, offsets, owners, left_stats, right_stats, left_root, right_root
        )
    return store(
        *exchange(
            n, grad_shards, offsets, owners, left_stats, right_stats, left_root, right_root
        )
    )


def solution(mesh):
    placed = (
        P("groups", "fsdp", None),
        P("groups"),
        P("groups"),
        P(("groups", "fsdp"), None, None),
        P(("groups", "fsdp"), None, None),
        P(("groups", "fsdp"), None, None),
        P(("groups", "fsdp"), None, None),
    )
    return jax.shard_map(
        body,
        mesh=mesh,
        in_specs=placed,
        out_specs=(
            P("groups", "fsdp", None),
            P(("groups", "fsdp"), None, None),
            P(("groups", "fsdp"), None, None),
        ),
        check_vma=False,
    )
```
